768 devices in a mesh: gx: 12 (over z), gy: 64 (over x, y, core).
Axes of the slice: x: 4, y: 8, z: 12, core: 2. Of those that a mesh axis runs over, the one named last changes fastest.
Arguments:
- pressure_now: float32 [384, 2048, 256], P('gx', 'gy'), may hold values from -6 to 6
- pressure_prev: float32 [384, 2048, 256], P('gx', 'gy'), may hold values from -6 to 6
- node_class: int32 [384, 2048, 256], P('gx', 'gy'), may hold values from 0 to 63, as said below
- admittance: float32 [8], replicated, may hold values from 0.05 to 1
Outputs:
- pressure_final: float32 [384, 2048, 256], P('gx', 'gy')
The draws below stay inside these ranges and needn't reach their ends.
Inputs may be any that keep to these rules, and one draw needn't show every extreme that they name: node_class is 0 for a solid cell; for an air cell it is 8 m + k, with m from 1 to 7 the wall class and k the number of its six neighbours inside the grid whose node_class is not 0. Solid cells come in whole bricks of 32 cells a side and as single cells.
All inputs are finite; a program needn't handle non-finite values.
Results may differ from the reference program's by a relative error of at most 0.00002.
Values sent between devices are 32-bit elements; how exact they have to be, the bound alone decides.
No kernel may reach another device: no remote copies, remote signals or barrier semaphores. Data moves between devices by JAX's collectives and lax.ppermute only.
A program may use at most 128 MiB of HBM per device.

```python
import math
import jax
import jax.numpy as jnp

BRICK = 32
STACK = 8
STEPS = 4
MATS = 8
NX = 384
NY = 2048
NZ = 256


def draw_node_class(key, part):
    key = jax.random.fold_in(key, 7)
    keys = jax.random.split(key, 4)
    columns = NX // BRICK
    rows_plan = NY // BRICK
    height = jax.random.randint(keys[0], (columns, rows_plan, 1), 1, STACK + 1)
    levels = jnp.arange(STACK, dtype=jnp.int32)[None, None, :]
    holes = jax.random.randint(keys[1], (columns, rows_plan, STACK), 0, 8)
    brick_open = ((levels < height) & (holes != 0)).astype(jnp.int32)
    opened = jnp.repeat(jnp.repeat(jnp.repeat(brick_open, BRICK, 0), BRICK, 1), BRICK, 2)
    speckle = jax.random.randint(keys[2], (NX, NY, NZ), 0, 16)
    opened = opened * (speckle != 0).astype(jnp.int32)
    padded = jnp.pad(opened, 1)
    counted = padded[2:, 1:-1, 1:-1] + padded[:-2, 1:-1, 1:-1]
    counted = counted + padded[1:-1, 2:, 1:-1] + padded[1:-1, :-2, 1:-1]
    counted = counted + padded[1:-1, 1:-1, 2:] + padded[1:-1, 1:-1, :-2]
    surface = jax.random.randint(keys[3], (NX, NY, NZ), 1, MATS)
    return (opened * (8 * surface + counted)).astype(jnp.int32)


def level_of(key, extent, cuts, smallest, largest):
    factor_of, own = 1.0, jax.random.fold_in(key, 6)
    for dim, blocks in cuts:
        heights = jnp.exp(jax.random.uniform(jax.random.fold_in(own, dim), (blocks,), jnp.float32, smallest / len(cuts), largest / len(cuts)))
        factor_of = factor_of * jnp.repeat(heights, extent[dim] // blocks).reshape([-1 if axis == dim else 1 for axis in range(len(extent))])
    return factor_of


def noise(key, shape, scale, reach, cuts=(), held_as=jnp.bfloat16):
    values = scale * jax.random.normal(key, shape, jnp.float32)
    if cuts:
        values = values * level_of(key, shape, cuts, -0.22, 0.18)
    return jnp.clip(values, -reach, reach).astype(held_as)


def setup_inputs(seed: int = 0) -> dict:
    seeds = jax.random.split(jax.random.key(seed), 5)
    pressure_now = noise(seeds[0], (NX, NY, NZ), 1.0, 6.0, ((0, 12), (1, 64)), jnp.float32)
    pressure_prev = noise(seeds[1], (NX, NY, NZ), 1.0, 6.0, ((0, 12), (1, 64)), jnp.float32)
    node_class = draw_node_class(jax.random.fold_in(seeds[4], 71), 0)
    admittance = jnp.clip(jnp.exp(jax.random.uniform(seeds[3], (MATS,), jnp.float32, math.log(0.05), math.log(1.0))), 0.05, 1.0)
    return {"pressure_now": pressure_now, "pressure_prev": pressure_prev, "node_class": node_class, "admittance": admittance}


THIRD = 1.0 / 3.0
ROOT_THIRD = 0.5773502691896258


def coefficients(node_class, admittance):
    surface = node_class // 8
    neighbours = (node_class % 8).astype(jnp.float32)
    filled = node_class > 0
    damping = ROOT_THIRD * (6.0 - neighbours) * admittance[surface] * 0.5
    factor = 1.0 / (1.0 + damping)
    weight_self = jnp.where(filled, (2.0 - neighbours * THIRD) * factor, jnp.float32(0.0))
    weight_side = jnp.where(filled, THIRD * factor, jnp.float32(0.0))
    weight_back = jnp.where(filled, (1.0 - damping) * factor, jnp.float32(0.0))
    return weight_self, weight_side, weight_back


def advance(current, earlier, weights):
    padded = jnp.pad(current, 1)
    summed = padded[2:, 1:-1, 1:-1] + padded[:-2, 1:-1, 1:-1]
    summed = summed + padded[1:-1, 2:, 1:-1] + padded[1:-1, :-2, 1:-1]
    summed = summed + padded[1:-1, 1:-1, 2:] + padded[1:-1, 1:-1, :-2]
    return weights[0] * current + weights[1] * summed - weights[2] * earlier


def reference(pressure_now, pressure_prev, node_class, admittance):
    weights = coefficients(node_class, admittance)
    filled = (node_class > 0).astype(jnp.float32)
    current = pressure_now * filled
    earlier = pressure_prev * filled
    for index in range(STEPS):
        following = advance(current, earlier, weights)
        earlier = current
        current = following
    return current
```

```python
import jax
import jax.numpy as jnp
from jax import lax
from jax.experimental import pallas as pl
from jax.experimental.pallas import tpu as pltpu
from jax.sharding import PartitionSpec as P

STEPS = 4
MATS = 8
TILE = 8
THIRD = 1.0 / 3.0
ROOT_THIRD = 0.5773502691896258
F32 = jnp.float32
VMEM = pl.BlockSpec(memory_space=pltpu.VMEM)
HBM = pl.BlockSpec(memory_space=pl.ANY)
SMEM = pl.BlockSpec(memory_space=pltpu.SMEM)
PARAMS = pltpu.CompilerParams(vmem_limit_bytes=40 * 1024 * 1024)


def cost(flops, moved):
    return pl.CostEstimate(flops=flops, bytes_accessed=moved, transcendentals=0)


def weights(code, table):
    bits = [(code & bit) != 0 for bit in (8, 16, 32)]
    level = [table[index] for index in range(MATS)]
    for bit in bits:
        level = [jnp.where(bit, high, low) for low, high in zip(level[::2], level[1::2])]
    missing = (6 - (code & 7)).astype(F32)
    damping = (ROOT_THIRD * 0.5) * missing * level[0]
    air = code > 0
    side = jnp.where(air, THIRD / (1.0 + damping), 0.0)
    return side, missing, air


def lateral(plane):
    rows, lanes = plane.shape
    lane = lax.broadcasted_iota(jnp.int32, plane.shape, 1)
    below = jnp.where(lane == 0, 0.0, pltpu.roll(plane, 1, 1))
    above = jnp.where(lane == lanes - 1, 0.0, pltpu.roll(plane, lanes - 1, 1))
    return (pltpu.roll(plane, 1, 0) + pltpu.roll(plane, rows - 1, 0)) + (below + above)


def step(plane, across, earlier, side, missing):
    return earlier + side * ((lateral(plane) + across) + (missing * plane - 6.0 * earlier))


def pack_rows(now_ref, prev_ref, class_ref, up_ref, down_ref, edge, code, sems):
    nx, ny, _ = now_ref.shape
    half = nx // 2
    copies = []
    for which, source in enumerate((now_ref, prev_ref, class_ref)):
        for end, start in enumerate((0, ny - TILE)):
            target = code.at[end] if which == 2 else edge.at[which, end]
            copy = pltpu.make_async_copy(
                source.at[:, pl.ds(start, TILE), :], target, sems.at[which, end]
            )
            copy.start()
            copies.append(copy)
    row = lax.broadcasted_iota(jnp.int32, (half, TILE, now_ref.shape[2]), 1)
    lower = row < TILE // 2
    for which in range(3):
        for end in range(2):
            copies[2 * which + end].wait()
            block = code[end].astype(F32) if which == 2 else edge[which, end]
            first, second = block[:half], block[half:]
            place = pl.ds(which * half, half)
            if end:
                up_ref[place] = jnp.where(lower, pltpu.roll(first, TILE // 2, 1), second)
            else:
                down_ref[place] = jnp.where(lower, first, pltpu.roll(second, TILE // 2, 1))


def own_state(table, now_ref, prev_ref, class_ref, c_ref, e_ref, s_ref, m_ref):
    def body(x, carry):
        side, missing, air = weights(class_ref[x], table)
        s_ref[x] = side
        m_ref[x] = missing
        c_ref[x] = jnp.where(air, now_ref[x], 0.0)
        e_ref[x] = jnp.where(air, prev_ref[x], 0.0)
        return carry

    lax.fori_loop(0, class_ref.shape[0], body, 0)


def joined(own, halo, x):
    return jnp.concatenate([own[x], halo[x]], axis=0)


def pack_planes(
    table, low_ref, high_ref, class_ref, c_ref, e_ref, s_ref, m_ref,
    ch_ref, eh_ref, sh_ref, mh_ref, left_ref, right_ref,
):
    nx = c_ref.shape[0]
    half = nx // 2
    row = lax.broadcasted_iota(jnp.int32, (TILE, c_ref.shape[2]), 0)
    lower = row < TILE // 2

    def body(x, carry):
        first, second = [], []
        for which in range(3):
            low, high = low_ref[which * half + x], high_ref[which * half + x]
            first.append(jnp.where(lower, high, pltpu.roll(low, TILE // 2, 0)))
            second.append(jnp.where(lower, pltpu.roll(high, TILE // 2, 0), low))
        for (now, prev, code), place in ((first, x), (second, x + half)):
            side, missing, air = weights(code.astype(jnp.int32), table)
            sh_ref[place] = side
            mh_ref[place] = missing
            ch_ref[place] = jnp.where(air, now, 0.0)
            eh_ref[place] = jnp.where(air, prev, 0.0)
        return carry

    lax.fori_loop(0, half, body, 0)
    own_rows = c_ref.shape[1]
    rows = own_rows + TILE
    for edge, inward, out_ref in ((0, 1, left_ref), (nx - 1, -1, right_ref)):
        place = [edge + inward * depth for depth in range(STEPS)]
        now = [joined(c_ref, ch_ref, x) for x in place]
        prev = [joined(e_ref, eh_ref, x) for x in place[:3]]
        side = [joined(s_ref, sh_ref, x) for x in place[:3]]
        missing = [joined(m_ref, mh_ref, x) for x in place[:3]]
        out_ref[pl.ds(0, rows)] = now[0]
        for taken in range(1, STEPS):
            following = []
            for depth in range(STEPS - taken):
                across = now[depth + 1] if depth == 0 else now[depth - 1] + now[depth + 1]
                following.append(step(now[depth], across, prev[depth], side[depth], missing[depth]))
            prev, now = now, following
            if taken < STEPS - 1:
                out_ref[pl.ds(taken * rows, rows)] = now[0]
            else:
                out_ref[pl.ds(4 * rows, own_rows)] = now[0][:own_rows]
        code = class_ref[place[0]].astype(F32)
        out_ref[pl.ds(3 * rows, own_rows)] = code
        which = 2 * half + (place[0] % half)
        low, high = low_ref[which], high_ref[which]
        if place[0] < half:
            halo = jnp.where(lower, high, pltpu.roll(low, TILE // 2, 0))
        else:
            halo = jnp.where(lower, pltpu.roll(high, TILE // 2, 0), low)
        out_ref[pl.ds(3 * rows + own_rows, TILE)] = halo
        out_ref[pl.ds(4 * rows + own_rows, own_rows)] = class_ref[place[1]].astype(F32)


def evolve(
    c_ref, e_ref, s_ref, m_ref, ch_ref, eh_ref, sh_ref, mh_ref, g_ref, odd, even
):
    nx, own_rows, _ = c_ref.shape
    rows = own_rows + TILE

    def sweep(read, read_earlier, write):
        def body(x, carry):
            before, plane = carry
            after = read(jnp.minimum(x + 1, nx - 1))
            across = before + jnp.where(x == nx - 1, 0.0, after)
            write(
                x,
                step(plane, across, read_earlier(x), joined(s_ref, sh_ref, x), joined(m_ref, mh_ref, x)),
            )
            return plane, after

        first = read(0)
        lax.fori_loop(0, nx, body, (jnp.zeros_like(first), first))

    def store(ref):
        def write(x, value):
            ref[x] = value

        return write

    def last(x, value):
        g_ref[x] = value[:own_rows]

    start = lambda x: joined(c_ref, ch_ref, x)
    sweep(start, lambda x: joined(e_ref, eh_ref, x), store(odd))
    sweep(lambda x: odd[x], start, store(even))
    sweep(lambda x: even[x], lambda x: odd[x], store(odd))
    sweep(lambda x: odd[x], lambda x: even[x], last)


def add_neighbours(
    table, from_left, from_right, left_ref, right_ref, s_ref, m_ref, sh_ref, mh_ref, g_ref, out_ref, edges, sems
):
    nx, own_rows, _ = s_ref.shape
    rows = own_rows + TILE
    inner = pltpu.make_async_copy(
        g_ref.at[pl.ds(STEPS, nx - 2 * STEPS)], out_ref.at[pl.ds(STEPS, nx - 2 * STEPS)], sems.at[0]
    )
    inner.start()
    copies = [inner]
    zeros = jnp.zeros((TILE, s_ref.shape[2]), F32)
    for end, (edge, inward, got, own) in enumerate(
        ((0, 1, from_left, left_ref), (nx - 1, -1, from_right, right_ref))
    ):
        place = [edge + inward * depth for depth in range(STEPS)]
        w0, w1, w2, w3 = [joined(s_ref, sh_ref, x) for x in place]
        k0, k1, k2 = [joined(m_ref, mh_ref, x) for x in place[:3]]
        fm0, fm1, fm2 = [got[pl.ds(t * rows, rows)] for t in range(3)]
        fo0, fo1, fo2 = [own[pl.ds(t * rows, rows)] for t in range(3)]
        fm3 = jnp.concatenate([got[pl.ds(4 * rows, own_rows)], zeros], axis=0)
        v1, j1, _ = weights(got[pl.ds(3 * rows, rows)].astype(jnp.int32), table)
        v2, _, _ = weights(got[pl.ds(4 * rows + own_rows, own_rows)].astype(jnp.int32), table)
        v2 = jnp.concatenate([v2, zeros], axis=0)
        a1 = v1 * fo0
        b1 = w0 * fm0
        a2 = v1 * ((lateral(a1) + j1 * a1) + (b1 + fo1))
        z2 = v2 * a1
        b2 = w0 * ((lateral(b1) + k0 * b1) + (a1 + fm1))
        c2 = w1 * b1
        a3 = a1 + v1 * ((lateral(a2) + j1 * a2) + ((z2 + b2) + (fo2 - 6.0 * a1)))
        b3 = b1 + w0 * ((lateral(b2) + k0 * b2) + ((a2 + c2) + (fm2 - 6.0 * b1)))
        c3 = w1 * ((lateral(c2) + k1 * c2) + b2)
        d3 = w2 * c2
        b4 = b2 + w0 * ((lateral(b3) + k0 * b3) + ((a3 + c3) + (fm3 - 6.0 * b2)))
        c4 = c2 + w1 * ((lateral(c3) + k1 * c3) + ((b3 + d3) - 6.0 * c2))
        d4 = w2 * ((lateral(d3) + k2 * d3) + c3)
        e4 = w3 * d3
        first = min(place)
        for x, value in zip(place, (b4, c4, d4, e4)):
            edges[end, x - first] = g_ref[x] + value[:own_rows]
        copy = pltpu.make_async_copy(edges.at[end], out_ref.at[pl.ds(first, STEPS)], sems.at[end + 1])
        copy.start()
        copies.append(copy)
    for copy in copies:
        copy.wait()


def shifted(array, axis, by):
    ends = lax.axis_size(axis) - 1
    pairs = [(i, i + 1) if by > 0 else (i + 1, i) for i in range(ends)]
    return lax.ppermute(array, axis, pairs)


def vmem(*shape):
    return jax.ShapeDtypeStruct(shape, F32)


def on_device(pressure_now, pressure_prev, node_class, admittance):
    nx, ny, nz = pressure_now.shape
    rows = ny + TILE
    cells = nx * ny * nz
    packed = vmem(3 * nx // 2, TILE, nz)
    up, down = pl.pallas_call(
        pack_rows,
        out_shape=[packed, packed],
        in_specs=[HBM] * 3,
        out_specs=[VMEM] * 2,
        scratch_shapes=[
            pltpu.VMEM((2, 2, nx, TILE, nz), F32),
            pltpu.VMEM((2, nx, TILE, nz), jnp.int32),
            pltpu.SemaphoreType.DMA((3, 2)),
        ],
        compiler_params=PARAMS,
        cost_estimate=cost(cells, 4 * cells),
        name="pack_rows",
    )(pressure_now, pressure_prev, node_class)
    low = shifted(up, "gy", 1)
    high = shifted(down, "gy", -1)
    own = pl.pallas_call(
        own_state,
        out_shape=[vmem(nx, ny, nz)] * 4,
        in_specs=[SMEM] + [VMEM] * 3,
        out_specs=[VMEM] * 4,
        compiler_params=PARAMS,
        cost_estimate=cost(30 * cells, 28 * cells),
        name="own_state",
    )(admittance, pressure_now, pressure_prev, node_class)
    plane = vmem(4 * rows + 2 * ny, nz)
    *halo, left, right = pl.pallas_call(
        pack_planes,
        out_shape=[vmem(nx, TILE, nz)] * 4 + [plane, plane],
        in_specs=[SMEM] + [VMEM] * 7,
        out_specs=[VMEM] * 6,
        compiler_params=PARAMS,
        cost_estimate=cost(10 * cells, 4 * cells),
        name="pack_planes",
    )(admittance, low, high, node_class, *own)
    from_left = shifted(right, "gx", 1)
    from_right = shifted(left, "gx", -1)
    free = pl.pallas_call(
        evolve,
        out_shape=vmem(nx, ny, nz),
        in_specs=[VMEM] * 8,
        out_specs=VMEM,
        scratch_shapes=[pltpu.VMEM((nx, rows, nz), F32)] * 2,
        compiler_params=PARAMS,
        cost_estimate=cost(60 * cells, 40 * cells),
        name="evolve",
    )(*own, *halo)
    return pl.pallas_call(
        add_neighbours,
        out_shape=vmem(nx, ny, nz),
        in_specs=[SMEM] + [VMEM] * 9,
        out_specs=HBM,
        scratch_shapes=[pltpu.VMEM((2, STEPS, ny, nz), F32), pltpu.SemaphoreType.DMA((3,))],
        compiler_params=PARAMS,
        cost_estimate=cost(10 * cells, 4 * cells),
        name="add_neighbours",
    )(admittance, from_left, from_right, left, right, own[2], own[3], halo[2], halo[3], free)


def solution(mesh):
    return jax.shard_map(
        on_device,
        mesh=mesh,
        in_specs=(P("gx", "gy", None), P("gx", "gy", None), P("gx", "gy", None), P()),
        out_specs=P("gx", "gy", None),
        check_vma=False,
    )
```

```python
import jax
import jax.numpy as jnp
from jax import lax
from jax.experimental import pallas as pl
from jax.experimental.pallas import tpu as pltpu
from jax.sharding import PartitionSpec as P

STEPS = 4
MATS = 8
TILE = 8
LANES = 128
CHUNKS = 4
THIRD = 1.0 / 3.0
ROOT_THIRD = 0.5773502691896258
F32 = jnp.float32
VMEM = pl.BlockSpec(memory_space=pltpu.VMEM)
HBM = pl.BlockSpec(memory_space=pltpu.HBM)
SMEM = pl.BlockSpec(memory_space=pltpu.SMEM)
PARAMS = pltpu.CompilerParams(vmem_limit_bytes=40 * 1024 * 1024)


def cost(flops, moved):
    return pl.CostEstimate(flops=flops, bytes_accessed=moved, transcendentals=0)


def weights(code, table):
    bits = [(code & bit) != 0 for bit in (8, 16, 32)]
    level = [table[index] for index in range(MATS)]
    for bit in bits:
        level = [jnp.where(bit, high, low) for low, high in zip(level[::2], level[1::2])]
    missing = (6 - (code & 7)).astype(F32)
    damping = (ROOT_THIRD * 0.5) * missing * level[0]
    air = code > 0
    side = jnp.where(air, THIRD / (1.0 + damping), 0.0)
    return side, missing, air


def lateral(plane):
    rows, lanes = plane.shape
    tiles = [plane[start : start + TILE] for start in range(0, rows, TILE)]
    row = lax.broadcasted_iota(jnp.int32, tiles[0].shape, 0)
    down = [pltpu.roll(tile, 1, 0) for tile in tiles]
    up = [pltpu.roll(tile, TILE - 1, 0) for tile in tiles]
    along_rows = jnp.concatenate(
        [
            jnp.where(row == 0, down[i - 1], down[i])
            + jnp.where(row == TILE - 1, up[(i + 1) % len(tiles)], up[i])
            for i in range(len(tiles))
        ],
        axis=0,
    )
    parts = [plane[:, start : start + LANES] for start in range(0, lanes, LANES)]
    lane = lax.broadcasted_iota(jnp.int32, parts[0].shape, 1)
    from_below = [0.0] + [pltpu.roll(part, 1, 1) for part in parts]
    from_above = [pltpu.roll(part, LANES - 1, 1) for part in parts] + [0.0]
    along_lanes = jnp.concatenate(
        [
            jnp.where(lane == 0, from_below[i], from_below[i + 1])
            + jnp.where(lane == LANES - 1, from_above[i + 1], from_above[i])
            for i in range(len(parts))
        ],
        axis=1,
    )
    return along_rows + along_lanes


def step(plane, across, earlier, side, missing):
    return earlier + side * ((lateral(plane) + across) + (missing * plane - 6.0 * earlier))


def pack_rows(now_ref, prev_ref, class_ref, cross_ref, chip_ref, edge, code, sems):
    odd = lax.axis_index("gy") % 2 == 1
    nx, ny, _ = now_ref.shape
    half = nx // 2
    copies = []
    for which, source in enumerate((now_ref, prev_ref, class_ref)):
        for end, start in enumerate((0, ny - TILE)):
            target = code.at[end] if which == 2 else edge.at[which, end]
            copy = pltpu.make_async_copy(
                source.at[:, pl.ds(start, TILE), :], target, sems.at[which, end]
            )
            copy.start()
            copies.append(copy)
    row = lax.broadcasted_iota(jnp.int32, (half, TILE, now_ref.shape[2]), 1)
    lower = row < TILE // 2
    for which in range(3):
        blocks = []
        for end in range(2):
            copies[2 * which + end].wait()
            block = code[end].astype(F32) if which == 2 else edge[which, end]
            blocks.append((block[:half], block[half:]))
        (first, second), (first_up, second_up) = blocks
        down = jnp.where(lower, first, pltpu.roll(second, TILE // 2, 1))
        up = jnp.where(lower, pltpu.roll(first_up, TILE // 2, 1), second_up)
        place = pl.ds(which * half, half)
        cross_ref[place] = jnp.where(odd, up, down)
        chip_ref[place] = jnp.where(odd, down, up)


def own_state(
    table, now_hbm, prev_hbm, class_hbm, c_ref, e_ref, s_ref, m_ref, class_ref, now, prev, sems
):
    nx = class_ref.shape[0]
    chunk = nx // CHUNKS
    copies = []
    for index in range(CHUNKS):
        place = pl.ds(index * chunk, chunk)
        for which, (source, target) in enumerate(
            ((class_hbm, class_ref), (now_hbm, now), (prev_hbm, prev))
        ):
            copy = pltpu.make_async_copy(source.at[place], target.at[place], sems.at[which, index])
            copy.start()
            copies.append(copy)

    def body(x, carry):
        side, missing, air = weights(class_ref[x], table)
        s_ref[x] = side
        m_ref[x] = missing
        c_ref[x] = jnp.where(air, now[x], 0.0)
        e_ref[x] = jnp.where(air, prev[x], 0.0)
        return carry

    for index in range(CHUNKS):
        for copy in copies[3 * index : 3 * index + 3]:
            copy.wait()
        lax.fori_loop(index * chunk, (index + 1) * chunk, body, 0, unroll=4)


def joined(own, halo, x):
    return jnp.concatenate([own[x], halo[x]], axis=0)


def pack_planes(
    table, cross_ref, chip_ref, class_ref, c_ref, e_ref, s_ref, m_ref,
    ch_ref, eh_ref, sh_ref, mh_ref, first_ref, second_ref,
):
    nx = c_ref.shape[0]
    odd_y = lax.axis_index("gy") % 2 == 1
    odd_x = lax.axis_index("gx") % 2 == 1

    def received(index):
        cross, chip = cross_ref[index], chip_ref[index]
        return jnp.where(odd_y, chip, cross), jnp.where(odd_y, cross, chip)

    half = nx // 2
    row = lax.broadcasted_iota(jnp.int32, (TILE, c_ref.shape[2]), 0)
    lower = row < TILE // 2

    def body(x, carry):
        first, second = [], []
        for which in range(3):
            low, high = received(which * half + x)
            first.append(jnp.where(lower, high, pltpu.roll(low, TILE // 2, 0)))
            second.append(jnp.where(lower, pltpu.roll(high, TILE // 2, 0), low))
        for (now, prev, code), place in ((first, x), (second, x + half)):
            side, missing, air = weights(code.astype(jnp.int32), table)
            sh_ref[place] = side
            mh_ref[place] = missing
            ch_ref[place] = jnp.where(air, now, 0.0)
            eh_ref[place] = jnp.where(air, prev, 0.0)
        return carry

    lax.fori_loop(0, half, body, 0)
    own_rows = c_ref.shape[1]
    rows = own_rows + TILE
    sides = []
    for edge, inward in ((0, 1), (nx - 1, -1)):
        out = {}
        place = [edge + inward * depth for depth in range(STEPS)]
        now = [joined(c_ref, ch_ref, x) for x in place]
        prev = [joined(e_ref, eh_ref, x) for x in place[:3]]
        side = [joined(s_ref, sh_ref, x) for x in place[:3]]
        missing = [joined(m_ref, mh_ref, x) for x in place[:3]]
        out[0] = now[0]
        for taken in range(1, STEPS):
            following = []
            for depth in range(STEPS - taken):
                across = now[depth + 1] if depth == 0 else now[depth - 1] + now[depth + 1]
                following.append(step(now[depth], across, prev[depth], side[depth], missing[depth]))
            prev, now = now, following
            if taken < STEPS - 1:
                out[taken * rows] = now[0]
            else:
                out[4 * rows] = now[0][:own_rows]
        code = class_ref[place[0]].astype(F32)
        out[3 * rows] = code
        which = 2 * half + (place[0] % half)
        low, high = received(which)
        if place[0] < half:
            halo = jnp.where(lower, high, pltpu.roll(low, TILE // 2, 0))
        else:
            halo = jnp.where(lower, pltpu.roll(high, TILE // 2, 0), low)
        out[3 * rows + own_rows] = halo
        out[4 * rows + own_rows] = class_ref[place[1]].astype(F32)
        sides.append(out)
    for start, left in sides[0].items():
        right = sides[1][start]
        place = pl.ds(start, left.shape[0])
        first_ref[place] = jnp.where(odd_x, right, left)
        second_ref[place] = jnp.where(odd_x, left, right)


def evolve(
    c_ref, e_ref, s_ref, m_ref, ch_ref, eh_ref, sh_ref, mh_ref, g_ref, odd, even
):
    nx, own_rows, _ = c_ref.shape
    rows = own_rows + TILE

    def sweep(read, read_earlier, write):
        planes = [read(x) for x in range(nx)]
        for x in range(nx):
            across = sum(planes[beside] for beside in (x - 1, x + 1) if 0 <= beside < nx)
            side, missing = joined(s_ref, sh_ref, x), joined(m_ref, mh_ref, x)
            write(x, step(planes[x], across, read_earlier(x), side, missing))

    def store(ref):
        def write(x, value):
            ref[x] = value

        return write

    def last(x, value):
        g_ref[x] = value[:own_rows]

    start = lambda x: joined(c_ref, ch_ref, x)
    sweep(start, lambda x: joined(e_ref, eh_ref, x), store(odd))
    sweep(lambda x: odd[x], start, store(even))
    sweep(lambda x: even[x], lambda x: odd[x], store(odd))
    sweep(lambda x: odd[x], lambda x: even[x], last)


def add_neighbours(
    table, got_first, got_second, first_ref, second_ref, s_ref, m_ref, sh_ref, mh_ref, g_ref, out_ref, edges, sems
):
    nx, own_rows, _ = s_ref.shape
    odd = lax.axis_index("gx") % 2 == 1
    rows = own_rows + TILE
    inner = pltpu.make_async_copy(
        g_ref.at[pl.ds(STEPS, nx - 2 * STEPS)], out_ref.at[pl.ds(STEPS, nx - 2 * STEPS)], sems.at[0]
    )
    inner.start()
    copies = [inner]
    zeros = jnp.zeros((TILE, s_ref.shape[2]), F32)
    for end, (edge, inward) in enumerate(((0, 1), (nx - 1, -1))):
        swapped = odd if end == 0 else jnp.logical_not(odd)

        def picked(first, second, start, count):
            place = pl.ds(start, count)
            return jnp.where(swapped, second[place], first[place])

        got = lambda start, count: picked(got_first, got_second, start, count)
        own = lambda start, count: picked(first_ref, second_ref, start, count)
        place = [edge + inward * depth for depth in range(STEPS)]
        w0, w1, w2, w3 = [joined(s_ref, sh_ref, x) for x in place]
        k0, k1, k2 = [joined(m_ref, mh_ref, x) for x in place[:3]]
        fm0, fm1, fm2 = [got(t * rows, rows) for t in range(3)]
        fo0, fo1, fo2 = [own(t * rows, rows) for t in range(3)]
        fm3 = jnp.concatenate([got(4 * rows, own_rows), zeros], axis=0)
        v1, j1, _ = weights(got(3 * rows, rows).astype(jnp.int32), table)
        v2, _, _ = weights(got(4 * rows + own_rows, own_rows).astype(jnp.int32), table)
        v2 = jnp.concatenate([v2, zeros], axis=0)
        a1 = v1 * fo0
        b1 = w0 * fm0
        a2 = v1 * ((lateral(a1) + j1 * a1) + (b1 + fo1))
        z2 = v2 * a1
        b2 = w0 * ((lateral(b1) + k0 * b1) + (a1 + fm1))
        c2 = w1 * b1
        a3 = a1 + v1 * ((lateral(a2) + j1 * a2) + ((z2 + b2) + (fo2 - 6.0 * a1)))
        b3 = b1 + w0 * ((lateral(b2) + k0 * b2) + ((a2 + c2) + (fm2 - 6.0 * b1)))
        c3 = w1 * ((lateral(c2) + k1 * c2) + b2)
        d3 = w2 * c2
        b4 = b2 + w0 * ((lateral(b3) + k0 * b3) + ((a3 + c3) + (fm3 - 6.0 * b2)))
        c4 = c2 + w1 * ((lateral(c3) + k1 * c3) + ((b3 + d3) - 6.0 * c2))
        d4 = w2 * ((lateral(d3) + k2 * d3) + c3)
        e4 = w3 * d3
        first = min(place)
        for x, value in zip(place, (b4, c4, d4, e4)):
            edges[end, x - first] = g_ref[x] + value[:own_rows]
        copy = pltpu.make_async_copy(edges.at[end], out_ref.at[pl.ds(first, STEPS)], sems.at[end + 1])
        copy.start()
        copies.append(copy)
    for copy in copies:
        copy.wait()


def swapped(array, axis, start):
    pairs = [(i, i + 1) for i in range(start, lax.axis_size(axis) - 1, 2)]
    return lax.ppermute(array, axis, pairs + [(j, i) for i, j in pairs])


def vmem(*shape):
    return jax.ShapeDtypeStruct(shape, F32)


def on_device(pressure_now, pressure_prev, node_class, admittance):
    nx, ny, nz = pressure_now.shape
    rows = ny + TILE
    cells = nx * ny * nz
    inputs = [pltpu.with_memory_space_constraint(x, pltpu.HBM) for x in (pressure_now, pressure_prev, node_class)]
    packed = vmem(3 * nx // 2, TILE, nz)
    cross, chip = pl.pallas_call(
        pack_rows,
        out_shape=[packed, packed],
        in_specs=[HBM] * 3,
        out_specs=[VMEM] * 2,
        scratch_shapes=[
            pltpu.VMEM((2, 2, nx, TILE, nz), F32),
            pltpu.VMEM((2, nx, TILE, nz), jnp.int32),
            pltpu.SemaphoreType.DMA((3, 2)),
        ],
        compiler_params=PARAMS,
        cost_estimate=cost(cells, 4 * cells),
        name="pack_rows",
    )(*inputs)
    cross = swapped(cross, "gy", 1)
    chip = swapped(chip, "gy", 0)
    *own, code = pl.pallas_call(
        own_state,
        out_shape=[vmem(nx, ny, nz)] * 4 + [jax.ShapeDtypeStruct((nx, ny, nz), jnp.int32)],
        in_specs=[SMEM] + [HBM] * 3,
        out_specs=[VMEM] * 5,
        scratch_shapes=[pltpu.VMEM((nx, ny, nz), F32)] * 2 + [pltpu.SemaphoreType.DMA((3, CHUNKS))],
        compiler_params=PARAMS,
        cost_estimate=cost(30 * cells, 28 * cells),
        name="own_state",
    )(admittance, *inputs)
    plane = vmem(4 * rows + 2 * ny, nz)
    *halo, first, second = pl.pallas_call(
        pack_planes,
        out_shape=[vmem(nx, TILE, nz)] * 4 + [plane, plane],
        in_specs=[SMEM] + [VMEM] * 7,
        out_specs=[VMEM] * 6,
        compiler_params=PARAMS,
        cost_estimate=cost(10 * cells, 4 * cells),
        name="pack_planes",
    )(admittance, cross, chip, code, *own)
    got_first = swapped(first, "gx", 1)
    got_second = swapped(second, "gx", 0)
    free = pl.pallas_call(
        evolve,
        out_shape=vmem(nx, ny, nz),
        in_specs=[VMEM] * 8,
        out_specs=VMEM,
        scratch_shapes=[pltpu.VMEM((nx, rows, nz), F32)] * 2,
        compiler_params=PARAMS,
        cost_estimate=cost(60 * cells, 40 * cells),
        name="evolve",
    )(*own, *halo)
    return pl.pallas_call(
        add_neighbours,
        out_shape=vmem(nx, ny, nz),
        in_specs=[SMEM] + [VMEM] * 9,
        out_specs=HBM,
        scratch_shapes=[pltpu.VMEM((2, STEPS, ny, nz), F32), pltpu.SemaphoreType.DMA((3,))],
        compiler_params=PARAMS,
        cost_estimate=cost(10 * cells, 4 * cells),
        name="add_neighbours",
    )(admittance, got_first, got_second, first, second, own[2], own[3], halo[2], halo[3], free)


def solution(mesh):
    return jax.shard_map(
        on_device,
        mesh=mesh,
        in_specs=(P("gx", "gy", None), P("gx", "gy", None), P("gx", "gy", None), P()),
        out_specs=P("gx", "gy", None),
        check_vma=False,
    )
```

```python
import functools

import jax
import jax.numpy as jnp
from jax import lax
from jax.experimental import pallas as pl
from jax.experimental.pallas import tpu as pltpu
from jax.sharding import PartitionSpec as P

STEPS = 4
MATS = 8
TILE = 8
LANES = 128
CHUNKS = 3
UP_FIRST = 2
THIRD = 1.0 / 3.0
ROOT_THIRD = 0.5773502691896258
F32 = jnp.float32
VMEM = pl.BlockSpec(memory_space=pltpu.VMEM)
HBM = pl.BlockSpec(memory_space=pltpu.HBM)
PARAMS = pltpu.CompilerParams(vmem_limit_bytes=40 * 1024 * 1024)


def cost(flops, moved):
    return pl.CostEstimate(flops=flops, bytes_accessed=moved, transcendentals=0)


def weights(code, table):
    bits = [(code & bit) != 0 for bit in (8, 16, 32)]
    level = [table[index : index + 1, :] for index in range(MATS)]
    for bit in bits:
        level = [jnp.where(bit, high, low) for low, high in zip(level[::2], level[1::2])]
    missing = (6 - (code & 7)).astype(F32)
    damping = (ROOT_THIRD * 0.5) * missing * level[0]
    air = code > 0
    side = jnp.where(air, THIRD / (1.0 + damping), 0.0)
    return side, missing, air


def lateral(plane):
    rows, lanes = plane.shape
    tiles = [plane[start : start + TILE] for start in range(0, rows, TILE)]
    row = lax.broadcasted_iota(jnp.int32, tiles[0].shape, 0)
    down = [pltpu.roll(tile, 1, 0) for tile in tiles]
    up = [pltpu.roll(tile, TILE - 1, 0) for tile in tiles]
    along_rows = jnp.concatenate(
        [
            jnp.where(row == 0, down[i - 1], down[i])
            + jnp.where(row == TILE - 1, up[(i + 1) % len(tiles)], up[i])
            for i in range(len(tiles))
        ],
        axis=0,
    )
    parts = [plane[:, start : start + LANES] for start in range(0, lanes, LANES)]
    lane = lax.broadcasted_iota(jnp.int32, parts[0].shape, 1)
    from_below = [0.0] + [pltpu.roll(part, 1, 1) for part in parts]
    from_above = [pltpu.roll(part, LANES - 1, 1) for part in parts] + [0.0]
    along_lanes = jnp.concatenate(
        [
            jnp.where(lane == 0, from_below[i], from_below[i + 1])
            + jnp.where(lane == LANES - 1, from_above[i + 1], from_above[i])
            for i in range(len(parts))
        ],
        axis=1,
    )
    return along_rows + along_lanes


def step(plane, across, earlier, side, missing):
    return earlier + side * ((lateral(plane) + across) + (missing * plane - 6.0 * earlier))


def rolled(tiles, shift):
    return pltpu.roll(tiles, shift % TILE, tiles.ndim - 2)


def pack_rows(
    admittance_ref, now_ref, prev_ref, class_ref,
    cross_ref, chip_ref, table_ref, now_ends, prev_ends, class_ends, edge, code, scalars, sems, end_sems, scalar_sem
):
    odd = lax.axis_index("gy") % 2 == 1
    nx, ny, nz = now_ref.shape
    copies = []
    for which, source in enumerate((now_ref, prev_ref, class_ref)):
        for end, start in enumerate((0, ny - TILE)):
            target = code.at[end] if which == 2 else edge.at[which, end]
            copy = pltpu.make_async_copy(
                source.at[:, pl.ds(start, TILE), :], target, sems.at[which, end]
            )
            copy.start()
            copies.append(copy)
    scalar_copy = pltpu.make_async_copy(admittance_ref, scalars, scalar_sem)
    scalar_copy.start()
    places = [(0, 0, STEPS), (nx - STEPS, STEPS, STEPS)]
    end_copies = fetch((now_ref, prev_ref, class_ref), (now_ends, prev_ends, class_ends), places, end_sems)
    row = lax.broadcasted_iota(jnp.int32, (nx, TILE, nz), 1)
    for copy in copies:
        copy.wait()
    classes = [code[end].astype(F32) for end in range(2)]
    now = [jnp.where(classes[end] > 0.0, edge[0, end], 0.0) for end in range(2)]
    down = jnp.where(row < 4, now[0], jnp.where(row < 7, rolled(edge[1, 0], 4), rolled(classes[0], 7)))
    up = jnp.where(row >= 4, now[1], jnp.where(row >= 1, rolled(edge[1, 1], 4), rolled(classes[1], 1)))
    cross_ref[pl.ds(0, nx)] = jnp.where(odd, up, down)
    chip_ref[pl.ds(0, nx)] = jnp.where(odd, down, up)
    some = nx // 4
    row = row[:some]
    for index in range(4):
        block = [classes[end][index * some : (index + 1) * some] for end in range(2)]
        block = rolled(block[0], 2 * index - 1), rolled(block[1], 2 * index - 5)
        if index == 0:
            down, up = block
        else:
            down = jnp.where(row < 2 * index, down, block[0])
            up = jnp.where(row < 2 * index, up, block[1])
    cross_ref[pl.ds(nx, some)] = jnp.where(odd, up, down)
    chip_ref[pl.ds(nx, some)] = jnp.where(odd, down, up)
    scalar_copy.wait()
    for index in range(MATS):
        table_ref[index : index + 1, :] = jnp.full((1, nz), scalars[index], F32)
    for copies in end_copies:
        for copy in copies:
            copy.wait()


def halo_tile(cross_ref, chip_ref, odd, x, nx):
    some = nx // 4
    index, shelf = x // some, nx + x % some
    row = lax.broadcasted_iota(jnp.int32, cross_ref.shape[1:], 0)
    cross, chip = cross_ref[x], chip_ref[x]
    low, high = jnp.where(odd, chip, cross), jnp.where(odd, cross, chip)
    cross, chip = cross_ref[shelf], chip_ref[shelf]
    low_more, high_more = jnp.where(odd, chip, cross), jnp.where(odd, cross, chip)
    now = jnp.where(row < 4, high, low)
    prev = rolled(jnp.where(row < 4, low, high), 4)
    more = jnp.where(row < 4, rolled(high_more, 1 - 2 * index), rolled(low_more, 5 - 2 * index))
    code = jnp.where(row == 0, rolled(high, 1), jnp.where(row == 7, rolled(low, 7), more))
    return now, prev, code


def put_state(table, place, now, prev, code, c_ref, e_ref, s_ref, m_ref, masked=False):
    side, missing, air = weights(code, table)
    s_ref[place] = side
    m_ref[place] = missing
    c_ref[place] = now if masked else jnp.where(air, now, 0.0)
    e_ref[place] = jnp.where(air, prev, 0.0)


def fetch(sources, targets, places, sems):
    copies = []
    for index, (start, to, count) in enumerate(places):
        copies.append([])
        for which, (source, target) in enumerate(zip(sources, targets)):
            copy = pltpu.make_async_copy(
                source.at[pl.ds(start, count)], target.at[pl.ds(to, count)], sems.at[which, index]
            )
            copy.start()
            copies[-1].append(copy)
    return copies


def joined(own, halo, x):
    return jnp.concatenate([own[x], halo[x]], axis=0)


def pack_planes(
    table, cross_ref, chip_ref, now_ends, prev_ends, class_ends,
    c_ref, e_ref, s_ref, m_ref, ch_ref, eh_ref, sh_ref, mh_ref, first_ref, second_ref, *, nx
):
    odd_y = lax.axis_index("gy") % 2 == 1
    up_first = lax.axis_index("gy") < UP_FIRST
    own_rows = now_ends.shape[1]
    row = lax.broadcasted_iota(jnp.int32, (TILE, c_ref.shape[2]), 0)
    sides = []
    for end in range(2):
        place = [7 - depth if end else depth for depth in range(STEPS)]
        for k in place:
            put_state(table, k, now_ends[k], prev_ends[k], class_ends[k], c_ref, e_ref, s_ref, m_ref)
            now, prev, code = halo_tile(cross_ref, chip_ref, odd_y, k + (nx - 2 * STEPS) * end, nx)
            if k == place[0]:
                class_halo = code
            put_state(table, k, now, prev, code.astype(jnp.int32), ch_ref, eh_ref, sh_ref, mh_ref, True)
        now = [joined(c_ref, ch_ref, k) for k in place]
        prev = [joined(e_ref, eh_ref, k) for k in place[:3]]
        side = [joined(s_ref, sh_ref, k) for k in place[:3]]
        missing = [joined(m_ref, mh_ref, k) for k in place[:3]]
        alone = [now[0]]
        for taken in range(1, STEPS):
            following = []
            for depth in range(STEPS - taken):
                across = now[depth + 1] if depth == 0 else now[depth - 1] + now[depth + 1]
                following.append(step(now[depth], across, prev[depth], side[depth], missing[depth]))
            prev, now = now, following
            alone.append(now[0])
        halos = [values[own_rows:] for values in alone]
        inner = (row == 3) | (row == 4)
        later = jnp.where(row == 3, rolled(halos[2], 3), rolled(halos[2], 5))
        middle = (row >= 2) & (row < 6)
        classes = jnp.where(row < 4, rolled(class_halo, 2), rolled(class_halo, 6))
        sides.append(
            [values[:own_rows] for values in alone]
            + [class_ends[k].astype(F32) for k in place[:2]]
            + [jnp.where(inner, later, halos[0]), jnp.where(middle, classes, halos[1])]
        )
    start = 0
    for left, right in zip(*sides):
        place = pl.ds(start, left.shape[0])
        first_ref[place] = jnp.where(up_first, right, left)
        second_ref[place] = jnp.where(up_first, left, right)
        start += left.shape[0]


def unpacked(read, own_rows):
    parts = [read(index * own_rows, own_rows) for index in range(6)]
    zeroth, first = read(6 * own_rows, TILE), read(6 * own_rows + TILE, TILE)
    row = lax.broadcasted_iota(jnp.int32, zeroth.shape, 0)
    second = jnp.where(row < 4, rolled(zeroth, 5), rolled(zeroth, 3))
    classes = jnp.where(row < 4, rolled(first, 6), rolled(first, 2))
    nothing = jnp.zeros_like(first)
    halos = [zeroth, first, second, nothing, classes, nothing]
    return [jnp.concatenate(pair, axis=0) for pair in zip(parts, halos)]


def evolve(
    table, now_hbm, prev_hbm, class_hbm, cross_ref, chip_ref,
    ce_ref, ee_ref, se_ref, me_ref, ceh_ref, eeh_ref, seh_ref, meh_ref,
    g_ref, odd, even, now, prev, code, c_ref, e_ref, s_ref, m_ref, ch_ref, eh_ref, sh_ref, mh_ref, sems
):
    nx, own_rows, _ = now_hbm.shape
    middle = nx - 2 * STEPS
    chunk = middle // CHUNKS
    places = [(STEPS + index * chunk, index * chunk, chunk) for index in range(CHUNKS)]
    copies = fetch((now_hbm, prev_hbm, class_hbm), (now, prev, code), places, sems)
    odd_y = lax.axis_index("gy") % 2 == 1
    for k in range(middle):
        halo_now, halo_prev, halo_code = halo_tile(cross_ref, chip_ref, odd_y, k + STEPS, nx)
        put_state(table, k, halo_now, halo_prev, halo_code.astype(jnp.int32), ch_ref, eh_ref, sh_ref, mh_ref, True)

    def body(k, carry):
        put_state(table, k, now[k], prev[k], code[k], c_ref, e_ref, s_ref, m_ref)
        return carry

    for index in range(CHUNKS):
        for copy in copies[index]:
            copy.wait()
        lax.fori_loop(index * chunk, (index + 1) * chunk, body, 0, unroll=4)

    def picked(edge, edge_halo, own, halo):
        def read(x):
            if x < STEPS:
                return joined(edge, edge_halo, x)
            if x >= nx - STEPS:
                return joined(edge, edge_halo, x - middle)
            return joined(own, halo, x - STEPS)

        return read

    start = picked(ce_ref, ceh_ref, c_ref, ch_ref)
    before = picked(ee_ref, eeh_ref, e_ref, eh_ref)
    sides = picked(se_ref, seh_ref, s_ref, sh_ref)
    missing = picked(me_ref, meh_ref, m_ref, mh_ref)

    def sweep(read, read_earlier, write):
        planes = [read(x) for x in range(nx)]
        for x in range(nx):
            across = sum(planes[beside] for beside in (x - 1, x + 1) if 0 <= beside < nx)
            write(x, step(planes[x], across, read_earlier(x), sides(x), missing(x)))

    def store(ref):
        def write(x, value):
            ref[x] = value

        return write

    def last(x, value):
        g_ref[x] = value[:own_rows]

    sweep(start, before, store(odd))
    sweep(lambda x: odd[x], start, store(even))
    sweep(lambda x: even[x], lambda x: odd[x], store(odd))
    sweep(lambda x: odd[x], lambda x: even[x], last)


def add_neighbours(
    table, got_first, got_second, first_ref, second_ref, s_ref, m_ref, sh_ref, mh_ref, g_ref, out_ref, edges, sems
):
    nx, own_rows, _ = g_ref.shape
    up_first = lax.axis_index("gy") < UP_FIRST
    chunk = (nx - 2 * STEPS) // CHUNKS
    copies = []
    for index in range(CHUNKS):
        place = pl.ds(STEPS + index * chunk, chunk)
        copies.append(pltpu.make_async_copy(g_ref.at[place], out_ref.at[place], sems.at[index]))
        copies[-1].start()
    for end in range(2):
        up = up_first if end else jnp.logical_not(up_first)

        def picked(yes, no):
            def read(start, count):
                place = pl.ds(start, count)
                return jnp.where(up, yes[place], no[place])

            return read

        fm0, fm1, fm2, fm3, code1, code2 = unpacked(picked(got_second, got_first), own_rows)
        fo0, fo1, fo2, _, _, _ = unpacked(picked(first_ref, second_ref), own_rows)
        place = [7 - depth if end else depth for depth in range(STEPS)]
        w0, w1, w2, w3 = [joined(s_ref, sh_ref, k) for k in place]
        k0, k1, k2 = [joined(m_ref, mh_ref, k) for k in place[:3]]
        v1, j1, _ = weights(code1.astype(jnp.int32), table)
        v2, _, _ = weights(code2.astype(jnp.int32), table)
        a1 = v1 * fo0
        b1 = w0 * fm0
        a2 = v1 * ((lateral(a1) + j1 * a1) + (b1 + fo1))
        z2 = v2 * a1
        b2 = w0 * ((lateral(b1) + k0 * b1) + (a1 + fm1))
        c2 = w1 * b1
        a3 = a1 + v1 * ((lateral(a2) + j1 * a2) + ((z2 + b2) + (fo2 - 6.0 * a1)))
        b3 = b1 + w0 * ((lateral(b2) + k0 * b2) + ((a2 + c2) + (fm2 - 6.0 * b1)))
        c3 = w1 * ((lateral(c2) + k1 * c2) + b2)
        d3 = w2 * c2
        b4 = b2 + w0 * ((lateral(b3) + k0 * b3) + ((a3 + c3) + (fm3 - 6.0 * b2)))
        c4 = c2 + w1 * ((lateral(c3) + k1 * c3) + ((b3 + d3) - 6.0 * c2))
        d4 = w2 * ((lateral(d3) + k2 * d3) + c3)
        e4 = w3 * d3
        for k, value in zip(place, (b4, c4, d4, e4)):
            edges[k] = g_ref[k + (nx - 2 * STEPS) * end] + value[:own_rows]
    for end in range(2):
        copy = pltpu.make_async_copy(
            edges.at[pl.ds(STEPS * end, STEPS)],
            out_ref.at[pl.ds((nx - STEPS) * end, STEPS)],
            sems.at[CHUNKS + end],
        )
        copy.start()
        copies.append(copy)
    for copy in copies:
        copy.wait()


def shifted(array, up_below):
    nx, ny = lax.axis_size("gx"), lax.axis_size("gy")
    pairs = []
    for j in range(ny):
        up = j < up_below if up_below >= 0 else j >= -up_below
        for i in range(nx - 1):
            low, high = i * ny + j, (i + 1) * ny + j
            pairs.append((low, high) if up else (high, low))
    return lax.ppermute(array, ("gx", "gy"), pairs)


def swapped(array, axis, start):
    pairs = [(i, i + 1) for i in range(start, lax.axis_size(axis) - 1, 2)]
    return lax.ppermute(array, axis, pairs + [(j, i) for i, j in pairs])


def vmem(*shape):
    return jax.ShapeDtypeStruct(shape, F32)


def on_device(pressure_now, pressure_prev, node_class, admittance):
    nx, ny, nz = pressure_now.shape
    rows = ny + TILE
    cells = nx * ny * nz
    middle = nx - 2 * STEPS
    inputs = [
        pltpu.with_memory_space_constraint(x, pltpu.HBM)
        for x in (admittance, pressure_now, pressure_prev, node_class)
    ]
    packed = vmem(nx + nx // 4, TILE, nz)
    edge = vmem(2 * STEPS, ny, nz)
    edge_code = jax.ShapeDtypeStruct(edge.shape, jnp.int32)
    cross, chip, table, *ends = pl.pallas_call(
        pack_rows,
        out_shape=[packed, packed, vmem(MATS, nz), edge, edge, edge_code],
        in_specs=[HBM] * 4,
        out_specs=[VMEM] * 6,
        scratch_shapes=[
            pltpu.VMEM((2, 2, nx, TILE, nz), F32),
            pltpu.VMEM((2, nx, TILE, nz), jnp.int32),
            pltpu.SMEM((MATS,), F32),
            pltpu.SemaphoreType.DMA((3, 2)),
            pltpu.SemaphoreType.DMA((3, 2)),
            pltpu.SemaphoreType.DMA,
        ],
        compiler_params=PARAMS,
        cost_estimate=cost(cells, 4 * cells),
        name="pack_rows",
    )(*inputs)
    cross = swapped(cross, "gy", 1)
    chip = swapped(chip, "gy", 0)
    plane = vmem(6 * ny + 2 * TILE, nz)
    packs = pl.pallas_call(
        functools.partial(pack_planes, nx=nx),
        out_shape=[edge] * 4 + [vmem(2 * STEPS, TILE, nz)] * 4 + [plane, plane],
        in_specs=[VMEM] * 6,
        out_specs=[VMEM] * 10,
        compiler_params=PARAMS,
        cost_estimate=cost(10 * cells, 4 * cells),
        name="pack_planes",
    )(table, cross, chip, *ends)
    edges, halos, (first, second) = packs[:4], packs[4:8], packs[8:]
    got_first = shifted(first, UP_FIRST)
    got_second = shifted(second, -UP_FIRST)
    free = pl.pallas_call(
        evolve,
        out_shape=vmem(nx, ny, nz),
        in_specs=[VMEM] + [HBM] * 3 + [VMEM] * 10,
        out_specs=VMEM,
        scratch_shapes=[pltpu.VMEM((nx, rows, nz), F32)] * 2
        + [pltpu.VMEM((middle, ny, nz), F32)] * 2
        + [pltpu.VMEM((middle, ny, nz), jnp.int32)]
        + [pltpu.VMEM((middle, ny, nz), F32)] * 4
        + [pltpu.VMEM((middle, TILE, nz), F32)] * 4
        + [pltpu.SemaphoreType.DMA((3, CHUNKS))],
        compiler_params=PARAMS,
        cost_estimate=cost(60 * cells, 40 * cells),
        name="evolve",
    )(table, *inputs[1:], cross, chip, *edges, *halos)
    return pl.pallas_call(
        add_neighbours,
        out_shape=vmem(nx, ny, nz),
        in_specs=[VMEM] * 10,
        out_specs=HBM,
        scratch_shapes=[pltpu.VMEM(edge.shape, F32), pltpu.SemaphoreType.DMA((CHUNKS + 2,))],
        compiler_params=PARAMS,
        cost_estimate=cost(10 * cells, 4 * cells),
        name="add_neighbours",
    )(table, got_first, got_second, first, second, edges[2], edges[3], halos[2], halos[3], free)


def solution(mesh):
    return jax.shard_map(
        on_device,
        mesh=mesh,
        in_specs=(P("gx", "gy", None), P("gx", "gy", None), P("gx", "gy", None), P()),
        out_specs=P("gx", "gy", None),
        check_vma=False,
    )
```

```python
import functools

import jax
import jax.numpy as jnp
from jax import lax
from jax.experimental import pallas as pl
from jax.experimental.pallas import tpu as pltpu
from jax.sharding import PartitionSpec as P

STEPS = 4
MATS = 8
TILE = 8
LANES = 128
CHUNKS = 4
PAIRED = 2
THIRD = 1.0 / 3.0
ROOT_THIRD = 0.5773502691896258
F32 = jnp.float32
VMEM = pl.BlockSpec(memory_space=pltpu.VMEM)
HBM = pl.BlockSpec(memory_space=pltpu.HBM)
PARAMS = pltpu.CompilerParams(vmem_limit_bytes=40 * 1024 * 1024)


def cost(flops, moved):
    return pl.CostEstimate(flops=flops, bytes_accessed=moved, transcendentals=0)


def weights(code, table):
    bits = [(code & bit) != 0 for bit in (8, 16, 32)]
    level = [table[index : index + 1, :] for index in range(MATS)]
    for bit in bits:
        level = [jnp.where(bit, high, low) for low, high in zip(level[::2], level[1::2])]
    missing = (6 - (code & 7)).astype(F32)
    damping = (ROOT_THIRD * 0.5) * missing * level[0]
    air = code > 0
    side = jnp.where(air, THIRD / (1.0 + damping), 0.0)
    return side, missing, air


def lateral(plane):
    rows, lanes = plane.shape
    tiles = [plane[start : start + TILE] for start in range(0, rows, TILE)]
    row = lax.broadcasted_iota(jnp.int32, tiles[0].shape, 0)
    down = [pltpu.roll(tile, 1, 0) for tile in tiles]
    up = [pltpu.roll(tile, TILE - 1, 0) for tile in tiles]
    along_rows = jnp.concatenate(
        [
            jnp.where(row == 0, down[i - 1], down[i])
            + jnp.where(row == TILE - 1, up[(i + 1) % len(tiles)], up[i])
            for i in range(len(tiles))
        ],
        axis=0,
    )
    parts = [plane[:, start : start + LANES] for start in range(0, lanes, LANES)]
    lane = lax.broadcasted_iota(jnp.int32, parts[0].shape, 1)
    from_below = [0.0] + [pltpu.roll(part, 1, 1) for part in parts]
    from_above = [pltpu.roll(part, LANES - 1, 1) for part in parts] + [0.0]
    along_lanes = jnp.concatenate(
        [
            jnp.where(lane == 0, from_below[i], from_below[i + 1])
            + jnp.where(lane == LANES - 1, from_above[i + 1], from_above[i])
            for i in range(len(parts))
        ],
        axis=1,
    )
    return along_rows + along_lanes


def step(plane, across, earlier, side, missing):
    return earlier + side * ((lateral(plane) + across) + (missing * plane - 6.0 * earlier))


def rolled(tiles, shift):
    return pltpu.roll(tiles, shift % TILE, tiles.ndim - 2)


def pack_rows(now_ref, prev_ref, class_ref, cross_ref, chip_ref, edge, code, sems):
    odd = lax.axis_index("gy") % 2 == 1
    nx, ny, nz = now_ref.shape
    copies = []
    for which, source in enumerate((now_ref, prev_ref, class_ref)):
        for end, start in enumerate((0, ny - TILE)):
            target = code.at[end] if which == 2 else edge.at[which, end]
            copy = pltpu.make_async_copy(
                source.at[:, pl.ds(start, TILE), :], target, sems.at[which, end]
            )
            copy.start()
            copies.append(copy)
    row = lax.broadcasted_iota(jnp.int32, (nx, TILE, nz), 1)
    for copy in copies:
        copy.wait()
    classes = [code[end].astype(F32) for end in range(2)]
    now = [jnp.where(classes[end] > 0.0, edge[0, end], 0.0) for end in range(2)]
    down = jnp.where(row < 4, now[0], jnp.where(row < 7, rolled(edge[1, 0], 4), rolled(classes[0], 7)))
    up = jnp.where(row >= 4, now[1], jnp.where(row >= 1, rolled(edge[1, 1], 4), rolled(classes[1], 1)))
    cross_ref[pl.ds(0, nx)] = jnp.where(odd, up, down)
    chip_ref[pl.ds(0, nx)] = jnp.where(odd, down, up)
    some = nx // 4
    row = row[:some]
    for index in range(4):
        block = [classes[end][index * some : (index + 1) * some] for end in range(2)]
        block = rolled(block[0], 2 * index - 1), rolled(block[1], 2 * index - 5)
        if index == 0:
            down, up = block
        else:
            down = jnp.where(row < 2 * index, down, block[0])
            up = jnp.where(row < 2 * index, up, block[1])
    cross_ref[pl.ds(nx, some)] = jnp.where(odd, up, down)
    chip_ref[pl.ds(nx, some)] = jnp.where(odd, down, up)


def halo_tile(cross_ref, chip_ref, odd, x, nx):
    some = nx // 4
    index, shelf = x // some, nx + x % some
    row = lax.broadcasted_iota(jnp.int32, cross_ref.shape[1:], 0)
    cross, chip = cross_ref[x], chip_ref[x]
    low, high = jnp.where(odd, chip, cross), jnp.where(odd, cross, chip)
    cross, chip = cross_ref[shelf], chip_ref[shelf]
    low_more, high_more = jnp.where(odd, chip, cross), jnp.where(odd, cross, chip)
    now = jnp.where(row < 4, high, low)
    prev = rolled(jnp.where(row < 4, low, high), 4)
    more = jnp.where(row < 4, rolled(high_more, 1 - 2 * index), rolled(low_more, 5 - 2 * index))
    code = jnp.where(row == 0, rolled(high, 1), jnp.where(row == 7, rolled(low, 7), more))
    return now, prev, code


def put_state(table, place, now, prev, code, c_ref, e_ref, s_ref, m_ref, masked=False):
    side, missing, air = weights(code, table)
    s_ref[place] = side
    m_ref[place] = missing
    c_ref[place] = now if masked else jnp.where(air, now, 0.0)
    e_ref[place] = jnp.where(air, prev, 0.0)


def fetch(sources, targets, places, sems):
    copies = []
    for index, (start, to, count) in enumerate(places):
        copies.append([])
        for which, (source, target) in enumerate(zip(sources, targets)):
            copy = pltpu.make_async_copy(
                source.at[pl.ds(start, count)], target.at[pl.ds(to, count)], sems.at[which, index]
            )
            copy.start()
            copies[-1].append(copy)
    return copies


def own_state(
    admittance_ref, now_ref, prev_ref, class_ref,
    table_ref, c_ref, e_ref, s_ref, m_ref, code, now, prev, scalars, sems, scalar_sem
):
    nx, _, nz = now_ref.shape
    scalar_copy = pltpu.make_async_copy(admittance_ref, scalars, scalar_sem)
    scalar_copy.start()
    chunk = nx // CHUNKS
    places = [(index * chunk, index * chunk, chunk) for index in range(CHUNKS)]
    copies = fetch((class_ref, now_ref, prev_ref), (code, now, prev), places, sems)
    scalar_copy.wait()
    for index in range(MATS):
        table_ref[index : index + 1, :] = jnp.full((1, nz), scalars[index], F32)

    def body(k, carry):
        put_state(table_ref, k, now[k], prev[k], code[k], c_ref, e_ref, s_ref, m_ref)
        return carry

    for index in range(CHUNKS):
        for copy in copies[index]:
            copy.wait()
        lax.fori_loop(index * chunk, (index + 1) * chunk, body, 0, unroll=4)


def pack_planes(
    table, cross_ref, chip_ref, code_ref, c_ref, e_ref, s_ref, m_ref,
    ch_ref, eh_ref, sh_ref, mh_ref, first_ref, second_ref
):
    odd_y = lax.axis_index("gy") % 2 == 1
    up_first, _ = ways()
    nx, own_rows, _ = c_ref.shape
    row = lax.broadcasted_iota(jnp.int32, (TILE, c_ref.shape[2]), 0)
    sides = []
    for end in range(2):
        place = [7 - depth if end else depth for depth in range(STEPS)]
        planes = [k + (nx - 2 * STEPS) * end for k in place]
        for k, x in zip(place, planes):
            now, prev, code = halo_tile(cross_ref, chip_ref, odd_y, x, nx)
            if k == place[0]:
                class_halo = code
            put_state(table, k, now, prev, code.astype(jnp.int32), ch_ref, eh_ref, sh_ref, mh_ref, True)
        both = lambda own, halo: [jnp.concatenate([own[x], halo[k]], axis=0) for k, x in zip(place, planes)]
        now, prev, side, missing = both(c_ref, ch_ref), both(e_ref, eh_ref), both(s_ref, sh_ref), both(m_ref, mh_ref)
        alone = [now[0]]
        for taken in range(1, STEPS):
            following = []
            for depth in range(STEPS - taken):
                across = now[depth + 1] if depth == 0 else now[depth - 1] + now[depth + 1]
                following.append(step(now[depth], across, prev[depth], side[depth], missing[depth]))
            prev, now = now, following
            alone.append(now[0])
        halos = [values[own_rows:] for values in alone]
        inner = (row == 3) | (row == 4)
        later = jnp.where(row == 3, rolled(halos[2], 3), rolled(halos[2], 5))
        middle = (row >= 2) & (row < 6)
        classes = jnp.where(row < 4, rolled(class_halo, 2), rolled(class_halo, 6))
        sides.append(
            [values[:own_rows] for values in alone]
            + [code_ref[x].astype(F32) for x in planes[:2]]
            + [jnp.where(inner, later, halos[0]), jnp.where(middle, classes, halos[1])]
        )
    start = 0
    for left, right in zip(*sides):
        place = pl.ds(start, left.shape[0])
        first_ref[place] = jnp.where(up_first, right, left)
        second_ref[place] = jnp.where(up_first, left, right)
        start += left.shape[0]


def unpacked(read, own_rows):
    parts = [read(index * own_rows, own_rows) for index in range(6)]
    zeroth, first = read(6 * own_rows, TILE), read(6 * own_rows + TILE, TILE)
    row = lax.broadcasted_iota(jnp.int32, zeroth.shape, 0)
    second = jnp.where(row < 4, rolled(zeroth, 5), rolled(zeroth, 3))
    classes = jnp.where(row < 4, rolled(first, 6), rolled(first, 2))
    nothing = jnp.zeros_like(first)
    halos = [zeroth, first, second, nothing, classes, nothing]
    return [jnp.concatenate(pair, axis=0) for pair in zip(parts, halos)]


def evolve(
    table, cross_ref, chip_ref, c_ref, e_ref, s_ref, m_ref, ceh_ref, eeh_ref, seh_ref, meh_ref,
    g_ref, odd, even, ch_ref, eh_ref, sh_ref, mh_ref
):
    nx, own_rows, _ = c_ref.shape
    middle = nx - 2 * STEPS
    odd_y = lax.axis_index("gy") % 2 == 1
    for k in range(middle):
        now, prev, code = halo_tile(cross_ref, chip_ref, odd_y, k + STEPS, nx)
        put_state(table, k, now, prev, code.astype(jnp.int32), ch_ref, eh_ref, sh_ref, mh_ref, True)

    def picked(own, edge_halo, halo):
        def read(x):
            if x < STEPS:
                beyond = edge_halo[x]
            elif x >= nx - STEPS:
                beyond = edge_halo[x - middle]
            else:
                beyond = halo[x - STEPS]
            return jnp.concatenate([own[x], beyond], axis=0)

        return read

    start = picked(c_ref, ceh_ref, ch_ref)
    before = picked(e_ref, eeh_ref, eh_ref)
    sides = picked(s_ref, seh_ref, sh_ref)
    missing = picked(m_ref, meh_ref, mh_ref)

    def sweep(read, read_earlier, write):
        planes = [read(x) for x in range(nx)]
        for x in range(nx):
            across = sum(planes[beside] for beside in (x - 1, x + 1) if 0 <= beside < nx)
            write(x, step(planes[x], across, read_earlier(x), sides(x), missing(x)))

    def store(ref):
        def write(x, value):
            ref[x] = value

        return write

    def last(x, value):
        g_ref[x] = value[:own_rows]

    sweep(start, before, store(odd))
    sweep(lambda x: odd[x], start, store(even))
    sweep(lambda x: even[x], lambda x: odd[x], store(odd))
    sweep(lambda x: odd[x], lambda x: even[x], last)


def add_neighbours(
    table, got_first, got_second, first_ref, second_ref, s_ref, m_ref, sh_ref, mh_ref, g_ref, out_ref, edges, sems
):
    nx, own_rows, _ = g_ref.shape
    up_first, right_first = ways()
    chunk = (nx - 2 * STEPS) // CHUNKS
    copies = []
    for index in range(CHUNKS):
        place = pl.ds(STEPS + index * chunk, chunk)
        copies.append(pltpu.make_async_copy(g_ref.at[place], out_ref.at[place], sems.at[index]))
        copies[-1].start()
    for end in range(2):

        def picked(is_right, first, second):
            first, second = (first, second) if end else (second, first)

            def read(start, count):
                place = pl.ds(start, count)
                return jnp.where(is_right, first[place], second[place])

            return read

        fm0, fm1, fm2, fm3, code1, code2 = unpacked(picked(right_first, got_first, got_second), own_rows)
        fo0, fo1, fo2, _, _, _ = unpacked(picked(up_first, first_ref, second_ref), own_rows)
        place = [7 - depth if end else depth for depth in range(STEPS)]
        planes = [k + (nx - 2 * STEPS) * end for k in place]
        both = lambda own, halo: [jnp.concatenate([own[x], halo[k]], axis=0) for k, x in zip(place, planes)]
        (w0, w1, w2, w3), (k0, k1, k2, _) = both(s_ref, sh_ref), both(m_ref, mh_ref)
        v1, j1, _ = weights(code1.astype(jnp.int32), table)
        v2, _, _ = weights(code2.astype(jnp.int32), table)
        a1 = v1 * fo0
        b1 = w0 * fm0
        a2 = v1 * ((lateral(a1) + j1 * a1) + (b1 + fo1))
        z2 = v2 * a1
        b2 = w0 * ((lateral(b1) + k0 * b1) + (a1 + fm1))
        c2 = w1 * b1
        a3 = a1 + v1 * ((lateral(a2) + j1 * a2) + ((z2 + b2) + (fo2 - 6.0 * a1)))
        b3 = b1 + w0 * ((lateral(b2) + k0 * b2) + ((a2 + c2) + (fm2 - 6.0 * b1)))
        c3 = w1 * ((lateral(c2) + k1 * c2) + b2)
        d3 = w2 * c2
        b4 = b2 + w0 * ((lateral(b3) + k0 * b3) + ((a3 + c3) + (fm3 - 6.0 * b2)))
        c4 = c2 + w1 * ((lateral(c3) + k1 * c3) + ((b3 + d3) - 6.0 * c2))
        d4 = w2 * ((lateral(d3) + k2 * d3) + c3)
        e4 = w3 * d3
        for k, value in zip(place, (b4, c4, d4, e4)):
            edges[k] = g_ref[k + (nx - 2 * STEPS) * end] + value[:own_rows]
    for end in range(2):
        copy = pltpu.make_async_copy(
            edges.at[pl.ds(STEPS * end, STEPS)],
            out_ref.at[pl.ds((nx - STEPS) * end, STEPS)],
            sems.at[CHUNKS + end],
        )
        copy.start()
        copies.append(copy)
    for copy in copies:
        copy.wait()


def ways():
    row = lax.axis_index("gy")
    pairs, odd = row < PAIRED, (lax.axis_index("gx") + row) % 2 == 0
    return pairs & jnp.logical_not(odd), jnp.logical_not(pairs & odd)


def moved(array, first):
    nx, ny = lax.axis_size("gx"), lax.axis_size("gy")
    pairs = []
    for i in range(nx - 1):
        for j in range(ny):
            low, high = i * ny + j, (i + 1) * ny + j
            if j < PAIRED:
                pairs += [(low, high), (high, low)] if ((i + j) % 2 == 1) == first else []
            else:
                pairs.append((high, low) if first else (low, high))
    return lax.ppermute(array, ("gx", "gy"), pairs)


def swapped(array, axis, start):
    pairs = [(i, i + 1) for i in range(start, lax.axis_size(axis) - 1, 2)]
    return lax.ppermute(array, axis, pairs + [(j, i) for i, j in pairs])


def vmem(*shape):
    return jax.ShapeDtypeStruct(shape, F32)


def on_device(pressure_now, pressure_prev, node_class, admittance):
    nx, ny, nz = pressure_now.shape
    rows = ny + TILE
    cells = nx * ny * nz
    middle = nx - 2 * STEPS
    inputs = [
        pltpu.with_memory_space_constraint(x, pltpu.HBM)
        for x in (admittance, pressure_now, pressure_prev, node_class)
    ]
    packed = vmem(nx + nx // 4, TILE, nz)
    cross, chip = pl.pallas_call(
        pack_rows,
        out_shape=[packed, packed],
        in_specs=[HBM] * 3,
        out_specs=[VMEM] * 2,
        scratch_shapes=[
            pltpu.VMEM((2, 2, nx, TILE, nz), F32),
            pltpu.VMEM((2, nx, TILE, nz), jnp.int32),
            pltpu.SemaphoreType.DMA((3, 2)),
        ],
        compiler_params=PARAMS,
        cost_estimate=cost(cells, 4 * cells),
        name="pack_rows",
    )(*inputs[1:])
    cross = swapped(cross, "gy", 1)
    chip = swapped(chip, "gy", 0)
    edge = vmem(2 * STEPS, ny, nz)
    whole = vmem(nx, ny, nz)
    code = jax.ShapeDtypeStruct(whole.shape, jnp.int32)
    table, *own, code = pl.pallas_call(
        own_state,
        out_shape=[vmem(MATS, nz)] + [whole] * 4 + [code],
        in_specs=[HBM] * 4,
        out_specs=[VMEM] * 6,
        scratch_shapes=[pltpu.VMEM(whole.shape, F32)] * 2
        + [pltpu.SMEM((MATS,), F32), pltpu.SemaphoreType.DMA((3, CHUNKS)), pltpu.SemaphoreType.DMA],
        compiler_params=PARAMS,
        cost_estimate=cost(20 * cells, 4 * cells),
        name="own_state",
    )(*inputs)
    plane = vmem(6 * ny + 2 * TILE, nz)
    packs = pl.pallas_call(
        pack_planes,
        out_shape=[vmem(2 * STEPS, TILE, nz)] * 4 + [plane, plane],
        in_specs=[VMEM] * 8,
        out_specs=[VMEM] * 6,
        compiler_params=PARAMS,
        cost_estimate=cost(10 * cells, 4 * cells),
        name="pack_planes",
    )(table, cross, chip, code, *own)
    halos, (first, second) = packs[:4], packs[4:]
    got_first = moved(first, True)
    got_second = moved(second, False)
    free = pl.pallas_call(
        evolve,
        out_shape=vmem(nx, ny, nz),
        in_specs=[VMEM] * 11,
        out_specs=VMEM,
        scratch_shapes=[pltpu.VMEM((nx, rows, nz), F32)] * 2 + [pltpu.VMEM((middle, TILE, nz), F32)] * 4,
        compiler_params=PARAMS,
        cost_estimate=cost(60 * cells, 40 * cells),
        name="evolve",
    )(table, cross, chip, *own, *halos)
    return pl.pallas_call(
        add_neighbours,
        out_shape=vmem(nx, ny, nz),
        in_specs=[VMEM] * 10,
        out_specs=HBM,
        scratch_shapes=[pltpu.VMEM(edge.shape, F32), pltpu.SemaphoreType.DMA((CHUNKS + 2,))],
        compiler_params=PARAMS,
        cost_estimate=cost(10 * cells, 4 * cells),
        name="add_neighbours",
    )(table, got_first, got_second, first, second, own[2], own[3], halos[2], halos[3], free)


def solution(mesh):
    return jax.shard_map(
        on_device,
        mesh=mesh,
        in_specs=(P("gx", "gy", None), P("gx", "gy", None), P("gx", "gy", None), P()),
        out_specs=P("gx", "gy", None),
        check_vma=False,
    )
```
